512 devices in a mesh: ta: 8 (over y_lo, core), ha: 8 (over y_hi, x), wa: 8 (over z).
Axes of the slice: x: 4, y: 8 (y_hi: 2, y_lo: 4; y = y_hi * 4 + y_lo), z: 8, core: 2. Of those that a mesh axis runs over, the one named last changes fastest.
Arguments:
- queries: bfloat16 [96, 32, 32, 1536], P('ta', 'ha', 'wa'), may hold values from -200 to 200
- keys: bfloat16 [96, 32, 32, 1536], P('ta', 'ha', 'wa'), may hold values from -8 to 8
- values: bfloat16 [96, 32, 32, 1536], P('ta', 'ha', 'wa'), may hold values from -6 to 6
Outputs:
- attended: bfloat16 [96, 32, 32, 1536], P('ta', 'ha', 'wa')
The draws below stay inside these ranges and needn't reach their ends.
All inputs are finite; a program needn't handle non-finite values.
Results may differ from the reference program's by a relative error of at most 0.0048.
Values may be sent and summed in bfloat16 or wider, within the bound.
A program may use at most 128 MiB of HBM per device.

```python
import jax
import jax.numpy as jnp
from jax import lax

HEADS = 12
HEAD_DIM = 128
TT = 6
TH = 4
TW = 4
HD = 1536
TILE = 96
NT = 96
NH = 32
NW = 32


def draw_queries(key, part):
    key = jax.random.fold_in(key, 5)
    own = jnp.clip(jax.random.normal(key, (NT, NH, NW, HEADS * HEAD_DIM), jnp.float32), -6.0, 6.0)
    return own.astype(jnp.bfloat16)


def draw_keys(key, part):
    key = jax.random.fold_in(key, 3)
    own = jnp.clip(jax.random.normal(key, (NT, NH, NW, HEADS * HEAD_DIM), jnp.float32), -6.0, 6.0)
    return own.astype(jnp.bfloat16)


def shard_levels(stream_key, shape, pieces, smallest, top_value):
    gain, own = 1.0, jax.random.fold_in(stream_key, 6)
    for position, shards_of in pieces:
        steps = jnp.exp(jax.random.uniform(jax.random.fold_in(own, position), (shards_of,), jnp.float32, smallest / len(pieces), top_value / len(pieces)))
        gain = gain * jnp.repeat(steps, shape[position] // shards_of).reshape([-1 if axis == position else 1 for axis in range(len(shape))])
    return gain


def normal_values(own_key, extent, width, most, cuts=(), kind=jnp.bfloat16):
    factor_of = shard_levels(own_key, extent, cuts, -0.22, 0.18) if cuts else 1.0
    entries = jax.random.normal(own_key, extent, jnp.float32) * width * factor_of
    return jnp.minimum(jnp.maximum(entries, -most), most).astype(kind)


def setup_inputs(seed: int = 0) -> dict:
    splits = jax.random.split(jax.random.key(seed), 4)
    queries = draw_queries(jax.random.fold_in(splits[3], 71), 0)
    keys = draw_keys(jax.random.fold_in(splits[3], 71), 0)
    values = normal_values(splits[2], (NT, NH, NW, HD), 1.0, 6.0, ((0, 8), (1, 8), (2, 8)))
    return {"queries": queries, "keys": keys, "values": values}


def attend(query_tile, key_window, value_window, mask_window):
    factor = HEAD_DIM ** -0.5
    scores = jnp.einsum("qhd,khd->hqk", query_tile.astype(jnp.float32), key_window.astype(jnp.float32)) * factor
    scores = jnp.where(mask_window[None, None, :], scores, -1e30)
    highest = jnp.max(scores, axis=2, keepdims=True)
    raised = jnp.exp(scores - highest)
    totals = jnp.sum(raised, axis=2)
    weights = raised.astype(jnp.bfloat16)
    blended = jnp.einsum("hqk,khd->qhd", weights.astype(jnp.float32), value_window.astype(jnp.float32))
    blended = blended / jnp.transpose(totals)[:, :, None]
    return blended.astype(jnp.bfloat16).reshape(TILE, HEADS * HEAD_DIM)


def reference(queries, keys, values):
    width_all = HEADS * HEAD_DIM
    margins = ((TT, TT), (TH, TH), (TW, TW), (0, 0))
    padded_keys = jnp.pad(keys, margins)
    padded_values = jnp.pad(values, margins)
    inside_mask = jnp.pad(jnp.ones((NT, NH, NW), jnp.int32), margins[:3]) > 0
    grid_time = NT // TT
    grid_rows = NH // TH
    grid_cols = NW // TW

    def one_tile(number):
        level = (number // (grid_rows * grid_cols)).astype(jnp.int32)
        across = ((number // grid_cols) % grid_rows).astype(jnp.int32)
        along = (number % grid_cols).astype(jnp.int32)
        zero = jnp.zeros((), jnp.int32)
        root = (level * TT, across * TH, along * TW, zero)
        query_tile = lax.dynamic_slice(queries, root, (TT, TH, TW, width_all)).reshape(TILE, HEADS, HEAD_DIM)
        key_window = lax.dynamic_slice(padded_keys, root, (3 * TT, 3 * TH, 3 * TW, width_all)).reshape(27 * TILE, HEADS, HEAD_DIM)
        value_window = lax.dynamic_slice(padded_values, root, (3 * TT, 3 * TH, 3 * TW, width_all)).reshape(27 * TILE, HEADS, HEAD_DIM)
        mask_window = lax.dynamic_slice(inside_mask, root[:3], (3 * TT, 3 * TH, 3 * TW)).reshape(27 * TILE)
        return attend(query_tile, key_window, value_window, mask_window)

    tiles = lax.map(one_tile, jnp.arange(grid_time * grid_rows * grid_cols, dtype=jnp.int32))
    tiles = tiles.reshape(grid_time, grid_rows, grid_cols, TT, TH, TW, width_all)
    return tiles.transpose(0, 3, 1, 4, 2, 5, 6).reshape(NT, NH, NW, width_all)
```

```python
import functools
import math

import jax
import jax.numpy as jnp
from jax import lax
from jax.experimental import pallas as pl
from jax.experimental.pallas import tpu as pltpu
from jax.sharding import PartitionSpec as P

HEAD_DIM = 128
TILE = 96
MESH = pl.DeviceIdType.MESH
SCALE = HEAD_DIM**-0.5 * math.log2(math.e)


def kernel(
    heads, q_hbm, kv_hbm, out_hbm,
    qb, kv, valid, osend, orecv, ssend, srecv, own_o, own_l, outb,
    lq, lkv, lout, xs, xr, ts, tr, qs, qr, os_, or_, ss, sr,
):
    t, h, w = lax.axis_index("ta"), lax.axis_index("ha"), lax.axis_index("wa")
    nt, nh, nw = lax.axis_size("ta"), lax.axis_size("ha"), lax.axis_size("wa")
    has_t = (t > 0, t < nt - 1)
    has_h = (h > 0, h < nh - 1)
    has_w = (w > 0, w < nw - 1)
    near_t = ((t - 1, h, w), (t + 1, h, w))
    near_h = ((t, h - 1, w), (t, h + 1, w))
    near_w = ((t, h, w - 1), (t, h, w + 1))

    def remote(src, dst, send, recv, device):
        return pltpu.make_async_remote_copy(src, dst, send, recv, device_id=device, device_id_type=MESH)

    def x_copy(j, d):
        return remote(kv_hbm.at[j], kv.at[j, 1:3, 0 if d else 2], xs.at[j, d], xr.at[j, 1 - d], near_h[d])

    def t_copy(j, d, hh):
        src = kv_hbm.at[j, d] if hh == 1 else kv.at[j, 1 + d, hh]
        return remote(src, kv.at[j, 0 if d else 3, hh], ts.at[j, d, hh], tr.at[j, 1 - d, hh], near_t[d])

    def q_copy(j, d):
        return remote(q_hbm.at[j], qb.at[j, :, 0 if d else 2], qs.at[j, d], qr.at[j, 1 - d], near_w[d])

    def o_copy(j, d):
        return remote(osend.at[j, d], orecv.at[j, 1 - d], os_.at[j, d], or_.at[j, 1 - d], near_w[d])

    def s_copy(j, d):
        return remote(ssend.at[j, d], srecv.at[j, 1 - d], ss.at[j, d], sr.at[j, 1 - d], near_w[d])

    def x_in(j, d):
        return remote(kv_hbm.at[j], kv.at[j, 1:3, 2 * d], xs.at[j, d], xr.at[j, d], near_h[d])

    def t_in(j, d, hh):
        return remote(kv_hbm.at[j, d], kv.at[j, 3 * d, hh], ts.at[j, d, hh], tr.at[j, d, hh], near_t[d])

    def q_in(j, d):
        return remote(q_hbm.at[j], qb.at[j, :, 2 * d], qs.at[j, d], qr.at[j, d], near_w[d])

    def o_in(j, d):
        return remote(osend.at[j, d], orecv.at[j, d], os_.at[j, d], or_.at[j, d], near_w[d])

    def s_in(j, d):
        return remote(ssend.at[j, d], srecv.at[j, d], ss.at[j, d], sr.at[j, d], near_w[d])

    def q_local(j):
        return pltpu.make_async_copy(q_hbm.at[j], qb.at[j, :, 1], lq.at[j])

    def kv_local(j):
        return pltpu.make_async_copy(kv_hbm.at[j], kv.at[j, 1:3, 1], lkv.at[j])

    def out_local(j):
        return pltpu.make_async_copy(outb.at[j], out_hbm.at[j], lout.at[j])

    barrier = pltpu.get_barrier_semaphore()
    count = jnp.int32(0)
    for has, near in ((has_t, near_t), (has_h, near_h), (has_w, near_w)):
        for d in (0, 1):
            pl.when(has[d])(
                lambda near=near, d=d: pl.semaphore_signal(
                    barrier, inc=1, device_id=near[d], device_id_type=MESH
                )
            )
            count += has[d].astype(jnp.int32)

    @pl.loop(0, heads)
    def _(j):
        kv_local(j).start()
        q_local(j).start()

    for tt in range(4):
        for hh in range(3):
            here = jnp.bool_(True)
            if tt in (0, 3):
                here = here & has_t[tt // 3]
            if hh in (0, 2):
                here = here & has_h[hh // 2]
            valid[tt, hh] = jnp.full((TILE, HEAD_DIM), here.astype(jnp.float32)).astype(jnp.bfloat16)
    for d in (0, 1):
        @pl.when(jnp.logical_not(has_w[d]))
        def _():
            qb[:, :, 2 * d] = jnp.zeros_like(qb[:, :, 2 * d])
            orecv[:, d] = jnp.zeros_like(orecv[:, d])
            srecv[:, d] = jnp.full_like(srecv[:, d], -1e30)

    pl.semaphore_wait(barrier, count)

    @pl.loop(0, heads)
    def _(j):
        for d in (0, 1):
            pl.when(has_h[d])(lambda: x_copy(j, d).start())
        for d in (0, 1):
            pl.when(has_t[d])(lambda: t_copy(j, d, 1).start())
        for d in (0, 1):
            pl.when(has_w[d])(lambda: q_copy(j, d).start())

    rows = lax.broadcasted_iota(jnp.int32, (TILE, HEAD_DIM), 0)
    lanes = lax.broadcasted_iota(jnp.int32, (TILE, HEAD_DIM), 1)
    diagonal = rows == lanes

    def forward(j):
        for e in (0, 1):
            @pl.when(has_h[e])
            def _():
                x_in(j, e).wait_recv()
                for d in (0, 1):
                    pl.when(has_t[d])(lambda: t_copy(j, d, 2 * e).start())

    def attend(j):
        kv_local(j).wait()
        q_local(j).wait()
        for d in (0, 1):
            pl.when(has_w[d])(lambda: q_in(j, d).wait_recv())
        for d in (0, 1):
            @pl.when(has_t[d])
            def _():
                t_in(j, d, 1).wait_recv()
                for e in (0, 1):
                    pl.when(has_h[e])(lambda: t_in(j, d, 2 * e).wait_recv())

        none = jnp.zeros((TILE, HEAD_DIM), jnp.bfloat16)
        for e in (0, 1):
            @pl.when(jnp.logical_not(has_h[e]))
            def _():
                for tt in range(4):
                    kv[j, tt, 2 * e, 0] = kv[j, 1 + tt // 2, 1, 0]
                    kv[j, tt, 2 * e, 1] = none
        for d in (0, 1):
            @pl.when(jnp.logical_not(has_t[d]))
            def _():
                for hh in range(3):
                    kv[j, 3 * d, hh, 0] = kv[j, 1 + d, 1, 0]
                    kv[j, 3 * d, hh, 1] = none

        for k in (0, 1):
            queries = qb[j, k].reshape(3 * TILE, HEAD_DIM)
            keys = kv[j, k : k + 3, :, 0].reshape(9 * TILE, HEAD_DIM)
            values = kv[j, k : k + 3, :, 1].reshape(9 * TILE, HEAD_DIM)
            counted = valid[k : k + 3].reshape(9 * TILE, HEAD_DIM)
            scores = lax.dot_general(
                queries, keys, (((1,), (1,)), ((), ())), preferred_element_type=jnp.float32
            )
            highest = jnp.max(scores, axis=1, keepdims=True)
            weights = jnp.exp2((scores - highest) * SCALE).astype(jnp.bfloat16)
            blended = jnp.dot(
                weights, jnp.concatenate([values, counted], axis=1), preferred_element_type=jnp.float32
            )
            totals = blended[:, HEAD_DIM:]
            part = blended[:, :HEAD_DIM] / totals
            level = highest * SCALE + jnp.log2(totals)
            own_o[j, k] = part[TILE : 2 * TILE]
            own_l[j, k] = level[TILE : 2 * TILE]
            for d in (0, 1):
                at = slice(2 * d * TILE, (2 * d + 1) * TILE)
                osend[j, d, k] = part[at].astype(jnp.bfloat16)
                ssend[j, d, k : k + 1] = jnp.sum(jnp.where(diagonal, level[at], 0.0), axis=0, keepdims=True)
        for d in (0, 1):
            @pl.when(has_w[d])
            def _():
                o_copy(j, d).start()
                s_copy(j, d).start()

    def combine(j):
        for d in (0, 1):
            @pl.when(has_w[d])
            def _():
                o_in(j, d).wait_recv()
                s_in(j, d).wait_recv()
        for k in (0, 1):
            levels = [own_l[j, k]]
            for d in (0, 1):
                row = jnp.broadcast_to(srecv[j, d, k : k + 1], (TILE, HEAD_DIM))
                levels.append(jnp.sum(jnp.where(diagonal, row, 0.0), axis=1, keepdims=True))
            top = jnp.maximum(jnp.maximum(levels[1], levels[2]), levels[0])
            shares = [jnp.exp2(level - top) for level in levels]
            mixed = shares[0] * own_o[j, k]
            for d in (0, 1):
                mixed += shares[1 + d] * orecv[j, d, k].astype(jnp.float32)
            outb[j, k] = (mixed / (shares[0] + shares[1] + shares[2])).astype(jnp.bfloat16)
        out_local(j).start()

    @pl.loop(0, heads + 2)
    def _(step):
        pl.when(step < heads)(lambda: forward(step))
        pl.when((step >= 1) & (step <= heads))(lambda: attend(step - 1))
        pl.when(step >= 2)(lambda: combine(step - 2))

    @pl.loop(0, heads)
    def _(j):
        out_local(j).wait()
        for d in (0, 1):
            @pl.when(has_h[d])
            def _():
                x_copy(j, d).wait_send()

            @pl.when(has_t[d])
            def _():
                t_copy(j, d, 1).wait_send()
                for e in (0, 1):
                    pl.when(has_h[e])(lambda: t_copy(j, d, 2 * e).wait_send())

            @pl.when(has_w[d])
            def _():
                q_copy(j, d).wait_send()
                o_copy(j, d).wait_send()
                s_copy(j, d).wait_send()


def body(queries, keys, values):
    frames, height, breadth, width_all = queries.shape
    heads = width_all // HEAD_DIM
    split = [x.reshape(2, TILE, heads, HEAD_DIM).transpose(2, 0, 1, 3) for x in (queries, keys, values)]
    pairs = jnp.stack(split[1:], axis=2)
    bf16, f32 = jnp.bfloat16, jnp.float32
    dma = pltpu.SemaphoreType.DMA
    result = pl.pallas_call(
        functools.partial(kernel, heads),
        out_shape=jax.ShapeDtypeStruct((heads, 2, TILE, HEAD_DIM), bf16),
        in_specs=[pl.BlockSpec(memory_space=pl.ANY)] * 2,
        out_specs=pl.BlockSpec(memory_space=pl.ANY),
        scratch_shapes=[
            pltpu.VMEM((heads, 2, 3, TILE, HEAD_DIM), bf16),
            pltpu.VMEM((heads, 4, 3, 2, TILE, HEAD_DIM), bf16),
            pltpu.VMEM((4, 3, TILE, HEAD_DIM), bf16),
            pltpu.VMEM((heads, 2, 2, TILE, HEAD_DIM), bf16),
            pltpu.VMEM((heads, 2, 2, TILE, HEAD_DIM), bf16),
            pltpu.VMEM((heads, 2, 8, HEAD_DIM), f32),
            pltpu.VMEM((heads, 2, 8, HEAD_DIM), f32),
            pltpu.VMEM((heads, 2, TILE, HEAD_DIM), f32),
            pltpu.VMEM((heads, 2, TILE, HEAD_DIM), f32),
            pltpu.VMEM((heads, 2, TILE, HEAD_DIM), bf16),
            dma((heads,)), dma((heads,)), dma((heads,)),
            dma((heads, 2)), dma((heads, 2)),
            dma((heads, 2, 3)), dma((heads, 2, 3)),
            dma((heads, 2)), dma((heads, 2)),
            dma((heads, 2)), dma((heads, 2)),
            dma((heads, 2)), dma((heads, 2)),
        ],
        compiler_params=pltpu.CompilerParams(
            collective_id=0, has_side_effects=True, vmem_limit_bytes=48 * 2**20
        ),
        name="window_attention",
    )(split[0], pairs)
    return result.transpose(1, 2, 0, 3).reshape(frames, height, breadth, width_all)


def solution(mesh):
    placed = (P("ta", "ha", "wa", None),) * 3
    return jax.shard_map(
        body, mesh=mesh, in_specs=placed, out_specs=P("ta", "ha", "wa", None), check_vma=False
    )
```

```python
import functools
import math

import jax
import jax.numpy as jnp
from jax import lax
from jax.experimental import pallas as pl
from jax.experimental.pallas import tpu as pltpu
from jax.sharding import PartitionSpec as P

HEAD_DIM = 128
TT, TH, TW = 6, 4, 4
TILE = TT * TH * TW
MESH = pl.DeviceIdType.MESH
SCALE = HEAD_DIM**-0.5 * math.log2(math.e)
AHEAD = 3
BEHIND = 3


def kernel(
    heads, q_hbm, k_hbm, v_hbm, outb,
    q_own, k_own, v_own, qb, kv, valid, osend, orecv, ssend, srecv, own_o, own_l,
    passing, load, es, xs, xr, ts, tr, qs, qr, os_, or_, ss, sr, ps, pr, fs, fr,
):
    t, h, w = lax.axis_index("ta"), lax.axis_index("ha"), lax.axis_index("wa")
    nt, nh, nw = lax.axis_size("ta"), lax.axis_size("ha"), lax.axis_size("wa")
    has_t = (t > 0, t < nt - 1)
    has_h = (h > 0, h < nh - 1)
    has_w = (w > 0, w < nw - 1)
    near_t = ((t - 1, h, w), (t + 1, h, w))
    near_h = ((t, h - 1, w), (t, h + 1, w))
    near_w = ((t, h, w - 1), (t, h, w + 1))
    low, high = nh // 2 - 1, nh // 2
    far = (h == high, h == low)
    is_far = (h == low) | (h == high)
    is_relay = (h == 0) | (h == nh - 1)
    relay = (t, jnp.where(h == low, 0, nh - 1), w)
    other_relay = (t, jnp.where(h == low, nh - 1, 0), w)
    relay_from = (t, jnp.where(h == 0, low, high), w)
    relay_to = (t, jnp.where(h == 0, high, low), w)
    far_slot = jnp.where(h == low, 2, 0)
    relay_slot = jnp.where(h == 0, 0, 2)

    off = lax.rem(t, 2)
    has_off = (off == 0) & has_t[0] | (off == 1) & has_t[1]
    is_inner = (h == low - 1) | (h == high + 1)
    inner_slot = jnp.where(h == low - 1, 0, 2)
    inner_to = (t, jnp.where(h == low - 1, low, high), w)

    def remote(src, dst, send, recv, device):
        return pltpu.make_async_remote_copy(src, dst, send, recv, device_id=device, device_id_type=MESH)

    def x_copy(j, d):
        return remote(kv.at[j, 1:3, 1], kv.at[j, 1:3, 0 if d else 2], xs.at[j, d], xr.at[j, 1 - d], near_h[d])

    def x_half(j, d):
        return remote(
            kv.at[j, 1, 1], kv.at[j, 1, 0 if d else 2], xs.at[j, d], xr.at[j, 1 - d], near_h[d]
        )

    def to_relay(j):
        return remote(kv.at[j, 2, 1], passing.at[j], ps.at[j], pr.at[j], relay)

    def relay_in(j):
        return remote(kv.at[j, 2, 1], passing.at[j], ps.at[j], pr.at[j], relay_from)

    def relay_out(j):
        return remote(passing.at[j], kv.at[j, 2, relay_slot], fs.at[j], fr.at[j], relay_to)

    def from_relay(j):
        return remote(passing.at[j], kv.at[j, 2, far_slot], fs.at[j], fr.at[j], other_relay)

    def t_copy(j, d, hh):
        return remote(kv.at[j, 1 + d, hh], kv.at[j, 0 if d else 3, hh], ts.at[j, d, hh], tr.at[j, 1 - d, hh], near_t[d])

    def edge_copy(j):
        return remote(
            kv.at[j, 3 * off, 1], kv.at[j, 3 * off, inner_slot], es.at[j], tr.at[j, off, inner_slot], inner_to
        )

    def q_copy(j, d):
        return remote(qb.at[j, :, 1], qb.at[j, :, 0 if d else 2], qs.at[j, d], qr.at[j, 1 - d], near_w[d])

    def o_copy(j, d):
        return remote(osend.at[j, d], orecv.at[j, 1 - d], os_.at[j, d], or_.at[j, 1 - d], near_w[d])

    def s_copy(j, d):
        return remote(ssend.at[j, d], srecv.at[j, 1 - d], ss.at[j, d], sr.at[j, 1 - d], near_w[d])

    def x_in(j, d):
        return remote(kv.at[j, 1:3, 1], kv.at[j, 1:3, 2 * d], xs.at[j, d], xr.at[j, d], near_h[d])

    def x_half_in(j, d):
        return remote(kv.at[j, 1, 1], kv.at[j, 1, 2 * d], xs.at[j, d], xr.at[j, d], near_h[d])

    def t_in(j, d, hh):
        return remote(kv.at[j, 1 + d, 1], kv.at[j, 3 * d, hh], ts.at[j, d, hh], tr.at[j, d, hh], (t + 2 * d - 1, h, w))

    def q_in(j, d):
        return remote(qb.at[j, :, 1], qb.at[j, :, 2 * d], qs.at[j, d], qr.at[j, d], near_w[d])

    def o_in(j, d):
        return remote(osend.at[j, d], orecv.at[j, d], os_.at[j, d], or_.at[j, d], near_w[d])

    def s_in(j, d):
        return remote(ssend.at[j, d], srecv.at[j, d], ss.at[j, d], sr.at[j, d], near_w[d])

    loads = [
        pltpu.make_async_copy(src, dst, load.at[i])
        for i, (src, dst) in enumerate(((k_hbm, k_own), (v_hbm, v_own), (q_hbm, q_own)))
    ]
    for copy in loads:
        copy.start()

    barrier = pltpu.get_barrier_semaphore()
    count = jnp.int32(0)
    for has, near in ((has_t, near_t), (has_h, near_h), (has_w, near_w)):
        for d in (0, 1):
            pl.when(has[d])(
                lambda near=near, d=d: pl.semaphore_signal(
                    barrier, inc=1, device_id=near[d], device_id_type=MESH
                )
            )
            count += has[d].astype(jnp.int32)
    for here, near in ((is_far, relay), (is_far, other_relay), (is_relay, relay_from), (is_relay, relay_to)):
        pl.when(here)(
            lambda near=near: pl.semaphore_signal(barrier, inc=1, device_id=near, device_id_type=MESH)
        )
        count += here.astype(jnp.int32)

    for tt in range(4):
        for hh in range(3):
            here = jnp.bool_(True)
            if tt in (0, 3):
                here = here & has_t[tt // 3]
            if hh in (0, 2):
                here = here & has_h[hh // 2]
            valid[tt, hh] = jnp.full((TILE, HEAD_DIM), here.astype(jnp.float32)).astype(jnp.bfloat16)
    for d in (0, 1):
        @pl.when(jnp.logical_not(has_w[d]))
        def _():
            qb[:, :, 2 * d] = jnp.zeros_like(qb[:, :, 2 * d])
            orecv[:, d] = jnp.zeros_like(orecv[:, d])
            srecv[:, d] = jnp.full_like(srecv[:, d], -1e30)

    def tiles(ref, j):
        at = pl.ds(pl.multiple_of(j * HEAD_DIM, HEAD_DIM), HEAD_DIM)
        return ref[:, :, :, at].reshape(2, TILE, HEAD_DIM)

    for copy in loads:
        copy.wait()

    none = jnp.zeros((TILE, HEAD_DIM), jnp.bfloat16)

    @pl.loop(0, heads)
    def _(j):
        kv[j, 1:3, 1, 0] = tiles(k_own, j)
        kv[j, 1:3, 1, 1] = tiles(v_own, j)
        qb[j, :, 1] = tiles(q_own, j)
        for e in (0, 1):
            @pl.when(jnp.logical_not(has_h[e]))
            def _():
                for tt in range(4):
                    kv[j, tt, 2 * e, 0] = kv[j, 1 + tt // 2, 1, 0]
                    kv[j, tt, 2 * e, 1] = none
        for d in (0, 1):
            @pl.when(jnp.logical_not(has_t[d]))
            def _():
                for hh in range(3):
                    kv[j, 3 * d, hh, 0] = kv[j, 1 + d, 1, 0]
                    kv[j, 3 * d, hh, 1] = none

    pl.semaphore_wait(barrier, count)

    def launch(j):
        for d in (0, 1):
            @pl.when(far[d])
            def _():
                to_relay(j).start()
                x_half(j, d).start()

            pl.when(has_h[d] & jnp.logical_not(far[d]))(lambda: x_copy(j, d).start())
        for d in (0, 1):
            pl.when(has_t[d])(lambda: t_copy(j, d, 1).start())
        for d in (0, 1):
            pl.when(has_w[d])(lambda: q_copy(j, d).start())

    pl.loop(0, AHEAD)(launch)

    rows = lax.broadcasted_iota(jnp.int32, (TILE, HEAD_DIM), 0)
    lanes = lax.broadcasted_iota(jnp.int32, (TILE, HEAD_DIM), 1)
    diagonal = rows == lanes

    def spreads(d, e):
        return has_t[d] & jnp.logical_not((off == d) & far[1 - e])

    def forward(j):
        @pl.when(is_relay)
        def _():
            relay_in(j).wait_recv()
            relay_out(j).start()

        @pl.when(is_inner & has_off)
        def _():
            t_in(j, off, 1).wait_recv()
            edge_copy(j).start()

        def spread(e):
            for d in (0, 1):
                pl.when(spreads(d, e))(lambda: t_copy(j, d, 2 * e).start())

        for e in (0, 1):
            @pl.when(has_h[e] & jnp.logical_not(far[e]))
            def _():
                x_in(j, e).wait_recv()
                spread(e)
        for e in (0, 1):
            @pl.when(far[e])
            def _():
                x_half_in(j, e).wait_recv()
                from_relay(j).wait_recv()
                spread(e)

    def attend(j):
        for d in (0, 1):
            pl.when(has_w[d])(lambda: q_in(j, d).wait_recv())
        for d in (0, 1):
            @pl.when(has_t[d])
            def _():
                pl.when(jnp.logical_not(is_inner & (off == d)))(lambda: t_in(j, d, 1).wait_recv())
                for e in (0, 1):
                    pl.when(has_h[e])(lambda: t_in(j, d, 2 * e).wait_recv())

        for k in (0, 1):
            queries = qb[j, k].reshape(3 * TILE, HEAD_DIM)
            keys = kv[j, k : k + 3, :, 0].reshape(9 * TILE, HEAD_DIM)
            values = kv[j, k : k + 3, :, 1].reshape(9 * TILE, HEAD_DIM)
            counted = valid[k : k + 3].reshape(9 * TILE, HEAD_DIM)
            scores = lax.dot_general(
                queries, keys, (((1,), (1,)), ((), ())), preferred_element_type=jnp.float32
            )
            highest = jnp.max(scores, axis=1, keepdims=True)
            weights = jnp.exp2((scores - highest) * SCALE).astype(jnp.bfloat16)
            blended = jnp.dot(
                weights, jnp.concatenate([values, counted], axis=1), preferred_element_type=jnp.float32
            )
            totals = blended[:, HEAD_DIM:]
            part = blended[:, :HEAD_DIM] / totals
            level = highest * SCALE + jnp.log2(totals)
            own_o[j, k] = part[TILE : 2 * TILE]
            own_l[j, k] = level[TILE : 2 * TILE]
            for d in (0, 1):
                at = slice(2 * d * TILE, (2 * d + 1) * TILE)
                osend[j, d, k] = part[at].astype(jnp.bfloat16)
                ssend[j, d, k : k + 1] = jnp.sum(jnp.where(diagonal, level[at], 0.0), axis=0, keepdims=True)
        for d in (0, 1):
            @pl.when(has_w[d])
            def _():
                o_copy(j, d).start()
                s_copy(j, d).start()

    def combine(j):
        for d in (0, 1):
            @pl.when(has_w[d])
            def _():
                o_in(j, d).wait_recv()
                s_in(j, d).wait_recv()
        for k in (0, 1):
            levels = [own_l[j, k]]
            for d in (0, 1):
                row = jnp.broadcast_to(srecv[j, d, k : k + 1], (TILE, HEAD_DIM))
                levels.append(jnp.sum(jnp.where(diagonal, row, 0.0), axis=1, keepdims=True))
            top = jnp.maximum(jnp.maximum(levels[1], levels[2]), levels[0])
            shares = [jnp.exp2(level - top) for level in levels]
            mixed = shares[0] * own_o[j, k]
            for d in (0, 1):
                mixed += shares[1 + d] * orecv[j, d, k].astype(jnp.float32)
            at = pl.ds(pl.multiple_of(j * HEAD_DIM, HEAD_DIM), HEAD_DIM)
            result = (mixed / (shares[0] + shares[1] + shares[2])).astype(jnp.bfloat16)
            outb[TT * k : TT * (k + 1), :, :, at] = result.reshape(TT, TH, TW, HEAD_DIM)

    @pl.loop(0, heads + BEHIND)
    def _(step):
        pl.when(step + AHEAD < heads)(lambda: launch(step + AHEAD))
        pl.when(step < heads)(lambda: forward(step))
        pl.when((step >= 1) & (step <= heads))(lambda: attend(step - 1))
        pl.when(step >= BEHIND)(lambda: combine(step - BEHIND))

    @pl.loop(0, heads)
    def _(j):
        pl.when(is_relay)(lambda: relay_out(j).wait_send())
        pl.when(is_inner & has_off)(lambda: edge_copy(j).wait_send())
        for d in (0, 1):
            @pl.when(far[d])
            def _():
                to_relay(j).wait_send()
                x_half(j, d).wait_send()

            pl.when(has_h[d] & jnp.logical_not(far[d]))(lambda: x_copy(j, d).wait_send())

            @pl.when(has_t[d])
            def _():
                t_copy(j, d, 1).wait_send()
                for e in (0, 1):
                    pl.when(has_h[e] & spreads(d, e))(lambda: t_copy(j, d, 2 * e).wait_send())

            @pl.when(has_w[d])
            def _():
                q_copy(j, d).wait_send()
                o_copy(j, d).wait_send()
                s_copy(j, d).wait_send()


def body(queries, keys, values):
    heads = queries.shape[3] // HEAD_DIM
    bf16, f32 = jnp.bfloat16, jnp.float32
    dma = pltpu.SemaphoreType.DMA
    own = pltpu.VMEM(queries.shape, jnp.bfloat16)
    return pl.pallas_call(
        functools.partial(kernel, heads),
        out_shape=jax.ShapeDtypeStruct(queries.shape, bf16),
        in_specs=[pl.BlockSpec(memory_space=pl.ANY)] * 3,
        out_specs=pl.BlockSpec(memory_space=pltpu.VMEM),
        scratch_shapes=[
            own, own, own,
            pltpu.VMEM((heads, 2, 3, TILE, HEAD_DIM), bf16),
            pltpu.VMEM((heads, 4, 3, 2, TILE, HEAD_DIM), bf16),
            pltpu.VMEM((4, 3, TILE, HEAD_DIM), bf16),
            pltpu.VMEM((heads, 2, 2, TILE, HEAD_DIM), bf16),
            pltpu.VMEM((heads, 2, 2, TILE, HEAD_DIM), bf16),
            pltpu.VMEM((heads, 2, 8, HEAD_DIM), f32),
            pltpu.VMEM((heads, 2, 8, HEAD_DIM), f32),
            pltpu.VMEM((heads, 2, TILE, HEAD_DIM), f32),
            pltpu.VMEM((heads, 2, TILE, HEAD_DIM), f32),
            pltpu.VMEM((heads, 2, TILE, HEAD_DIM), bf16),
            dma((3,)), dma((heads,)),
            dma((heads, 2)), dma((heads, 2)),
            dma((heads, 2, 3)), dma((heads, 2, 3)),
            dma((heads, 2)), dma((heads, 2)),
            dma((heads, 2)), dma((heads, 2)),
            dma((heads, 2)), dma((heads, 2)),
            dma((heads,)), dma((heads,)), dma((heads,)), dma((heads,)),
        ],
        compiler_params=pltpu.CompilerParams(
            collective_id=0, has_side_effects=True, vmem_limit_bytes=63 * 2**20
        ),
        name="window_attention",
    )(queries, keys, values)


def solution(mesh):
    placed = (P("ta", "ha", "wa", None),) * 3
    return jax.shard_map(
        body, mesh=mesh, in_specs=placed, out_specs=P("ta", "ha", "wa", None), check_vma=False
    )
```

```python
import functools
import math

import jax
import jax.numpy as jnp
from jax import lax
from jax.experimental import pallas as pl
from jax.experimental.pallas import tpu as pltpu
from jax.sharding import PartitionSpec as P

HEAD_DIM = 128
TT, TH, TW = 6, 4, 4
TILE = TT * TH * TW
MESH = pl.DeviceIdType.MESH
SCALE = HEAD_DIM**-0.5 * math.log2(math.e)
SHARES = (32, 32, 16, 16)
RELAYS = (0, 2, 1)
INNER = False
GROUP = 2
AHEAD = 2
FAR_AHEAD = 3
LEAD = 1
BEHIND = 3


def kernel(
    groups, q_hbm, k_hbm, v_hbm, outb,
    q_own, k_own, v_own, qb, kv, valid, osend, orecv, ssend, srecv, own_o, own_l,
    passing, load, es, xs, xr, ts, tr, qs, qr, os_, or_, ss, sr, ps, pr, fs, fr,
):
    t, h, w = lax.axis_index("ta"), lax.axis_index("ha"), lax.axis_index("wa")
    nt, nh, nw = lax.axis_size("ta"), lax.axis_size("ha"), lax.axis_size("wa")
    has_t = (t > 0, t < nt - 1)
    has_h = (h > 0, h < nh - 1)
    has_w = (w > 0, w < nw - 1)
    near_t = ((t - 1, h, w), (t + 1, h, w))
    near_h = ((t, h - 1, w), (t, h + 1, w))
    near_w = ((t, h, w - 1), (t, h, w + 1))
    low, high = nh // 2 - 1, nh // 2
    far = (h == high, h == low)
    is_far = (h == low) | (h == high)
    lower = h <= low
    relays = [(t, jnp.where(h == low, r, nh - 1 - r), w) for r in RELAYS]
    other_relays = [(t, jnp.where(h == low, nh - 1 - r, r), w) for r in RELAYS]
    is_relay = [(h == r) | (h == nh - 1 - r) for r in RELAYS]
    relay_from = (t, jnp.where(lower, low, high), w)
    relay_to = (t, jnp.where(lower, high, low), w)
    shares = [pl.ds(sum(SHARES[:i]), size) for i, size in enumerate(SHARES)]
    far_slot = jnp.where(h == low, 2, 0)
    relay_slot = jnp.where(lower, 0, 2)

    off = lax.rem(t, 2)
    has_off = (off == 0) & has_t[0] | (off == 1) & has_t[1]
    is_inner = (h == low - 1) | (h == high + 1)
    inner_slot = jnp.where(h == low - 1, 0, 2)
    inner_to = (t, jnp.where(h == low - 1, low, high), w)

    def remote(src, dst, send, recv, device):
        return pltpu.make_async_remote_copy(src, dst, send, recv, device_id=device, device_id_type=MESH)

    def nth(j):
        return 0 if isinstance(j, slice) else j

    def x_copy(j, d):
        return remote(kv.at[j, :, 1:3, 1], kv.at[j, :, 1:3, 0 if d else 2], xs.at[d], xr.at[nth(j), 1 - d], near_h[d])

    def x_half(j, d):
        return remote(
            kv.at[j, :, 1:3, 1, :, shares[0]], kv.at[j, :, 1:3, 0 if d else 2, :, shares[0]],
            xs.at[d], xr.at[nth(j), 1 - d], near_h[d],
        )

    def held(j, i):
        return passing.at[j, :, :, :, pl.ds(0, SHARES[1 + i])]

    def to_relay(j, i):
        return remote(kv.at[j, :, 1:3, 1, :, shares[1 + i]], held(j, i), ps.at[i], pr.at[nth(j)], relays[i])

    def relay_in(j, i):
        return remote(kv.at[j, :, 1:3, 1, :, shares[1 + i]], held(j, i), ps.at[i], pr.at[nth(j)], relay_from)

    def relay_out(j, i):
        return remote(
            held(j, i), kv.at[j, :, 1:3, relay_slot, :, shares[1 + i]], fs.at[i], fr.at[nth(j), i], relay_to
        )

    def from_relay(j, i):
        return remote(
            held(j, i), kv.at[j, :, 1:3, far_slot, :, shares[1 + i]], fs.at[i], fr.at[nth(j), i], other_relays[i]
        )

    def t_copy(j, d, hh):
        return remote(kv.at[j, :, 1 + d, hh], kv.at[j, :, 0 if d else 3, hh], ts.at[d, hh], tr.at[nth(j), 1 - d, hh], near_t[d])

    def edge_copy(j):
        return remote(
            kv.at[j, :, 3 * off, 1], kv.at[j, :, 3 * off, inner_slot], es.at[0], tr.at[nth(j), off, inner_slot], inner_to
        )

    def q_copy(j, d):
        return remote(qb.at[j, :, :, 1], qb.at[j, :, :, 0 if d else 2], qs.at[d], qr.at[nth(j), 1 - d], near_w[d])

    def o_copy(j, d):
        return remote(osend.at[j, d], orecv.at[j, 1 - d], os_.at[d], or_.at[nth(j), 1 - d], near_w[d])

    def s_copy(j, d):
        return remote(ssend.at[j, d], srecv.at[j, 1 - d], ss.at[d], sr.at[nth(j), 1 - d], near_w[d])

    def x_in(j, d):
        return remote(kv.at[j, :, 1:3, 1], kv.at[j, :, 1:3, 2 * d], xs.at[d], xr.at[nth(j), d], near_h[d])

    def x_half_in(j, d):
        return remote(
            kv.at[j, :, 1:3, 1, :, shares[0]], kv.at[j, :, 1:3, 2 * d, :, shares[0]],
            xs.at[d], xr.at[nth(j), d], near_h[d],
        )

    def t_in(j, d, hh):
        return remote(kv.at[j, :, 1 + d, 1], kv.at[j, :, 3 * d, hh], ts.at[d, hh], tr.at[nth(j), d, hh], (t + 2 * d - 1, h, w))

    def q_in(j, d):
        return remote(qb.at[j, :, :, 1], qb.at[j, :, :, 2 * d], qs.at[d], qr.at[nth(j), d], near_w[d])

    def o_in(j, d):
        return remote(osend.at[j, d], orecv.at[j, d], os_.at[d], or_.at[nth(j), d], near_w[d])

    def s_in(j, d):
        return remote(ssend.at[j, d], srecv.at[j, d], ss.at[d], sr.at[nth(j), d], near_w[d])

    loads = [
        pltpu.make_async_copy(src, dst, load.at[i])
        for i, (src, dst) in enumerate(((k_hbm, k_own), (v_hbm, v_own), (q_hbm, q_own)))
    ]
    for copy in loads:
        copy.start()

    barrier = pltpu.get_barrier_semaphore()
    count = jnp.int32(0)
    for has, near in ((has_t, near_t), (has_h, near_h), (has_w, near_w)):
        for d in (0, 1):
            pl.when(has[d])(
                lambda near=near, d=d: pl.semaphore_signal(
                    barrier, inc=1, device_id=near[d], device_id_type=MESH
                )
            )
            count += has[d].astype(jnp.int32)
    greet = [(is_far, r) for r in relays + other_relays]
    greet += [(here, near) for here in is_relay for near in (relay_from, relay_to)]
    for here, near in greet:
        pl.when(here)(
            lambda near=near: pl.semaphore_signal(barrier, inc=1, device_id=near, device_id_type=MESH)
        )
        count += here.astype(jnp.int32)

    for tt in range(4):
        for hh in range(3):
            here = jnp.bool_(True)
            if tt in (0, 3):
                here = here & has_t[tt // 3]
            if hh in (0, 2):
                here = here & has_h[hh // 2]
            valid[tt, hh] = jnp.full((TILE, HEAD_DIM), here.astype(jnp.float32)).astype(jnp.bfloat16)
    for d in (0, 1):
        @pl.when(jnp.logical_not(has_w[d]))
        def _():
            qb[:, :, :, 2 * d] = jnp.zeros_like(qb[:, :, :, 2 * d])
            orecv[:, d] = jnp.zeros_like(orecv[:, d])
            srecv[:, d] = jnp.full_like(srecv[:, d], -1e30)

    def tiles(ref, j):
        at = pl.ds(pl.multiple_of(j * HEAD_DIM, HEAD_DIM), HEAD_DIM)
        return ref[:, :, :, at].reshape(2, TILE, HEAD_DIM)

    for copy in loads:
        copy.wait()

    none = jnp.zeros((TILE, HEAD_DIM), jnp.bfloat16)

    @pl.loop(0, groups)
    def _(j):
        @pl.loop(0, GROUP)
        def _(g):
            kv[j, g, 1:3, 1, 0] = tiles(k_own, j * GROUP + g)
            kv[j, g, 1:3, 1, 1] = tiles(v_own, j * GROUP + g)
            qb[j, g, :, 1] = tiles(q_own, j * GROUP + g)
            for e in (0, 1):
                @pl.when(jnp.logical_not(has_h[e]))
                def _():
                    for tt in range(4):
                        kv[j, g, tt, 2 * e, 0] = kv[j, g, 1 + tt // 2, 1, 0]
                        kv[j, g, tt, 2 * e, 1] = none
            for d in (0, 1):
                @pl.when(jnp.logical_not(has_t[d]))
                def _():
                    for hh in range(3):
                        kv[j, g, 3 * d, hh, 0] = kv[j, g, 1 + d, 1, 0]
                        kv[j, g, 3 * d, hh, 1] = none

    pl.semaphore_wait(barrier, count)

    def launch_far(j):
        for d in (0, 1):
            @pl.when(far[d])
            def _():
                for i in range(len(RELAYS)):
                    to_relay(j, i).start()
                x_half(j, d).start()

    def launch(j):
        for d in (0, 1):
            pl.when(has_h[d] & jnp.logical_not(far[d]))(lambda: x_copy(j, d).start())
        for d in (0, 1):
            pl.when(has_t[d])(lambda: t_copy(j, d, 1).start())
        for d in (0, 1):
            pl.when(has_w[d])(lambda: q_copy(j, d).start())

    pl.loop(0, FAR_AHEAD)(launch_far)
    pl.loop(0, AHEAD)(launch)

    rows = lax.broadcasted_iota(jnp.int32, (TILE, HEAD_DIM), 0)
    lanes = lax.broadcasted_iota(jnp.int32, (TILE, HEAD_DIM), 1)
    diagonal = rows == lanes

    def spreads(d, e):
        return has_t[d] & jnp.logical_not((off == d) & far[1 - e]) if INNER else has_t[d]

    def pass_on(j):
        for i in range(len(RELAYS)):
            @pl.when(is_relay[i])
            def _():
                relay_in(j, i).wait_recv()
                relay_out(j, i).start()

    def forward(j):

        if INNER:
            @pl.when(is_inner & has_off)
            def _():
                t_in(j, off, 1).wait_recv()
                edge_copy(j).start()

        def spread(e):
            for d in (0, 1):
                pl.when(spreads(d, e))(lambda: t_copy(j, d, 2 * e).start())

        for e in (0, 1):
            @pl.when(has_h[e] & jnp.logical_not(far[e]))
            def _():
                x_in(j, e).wait_recv()
                spread(e)
        for e in (0, 1):
            @pl.when(far[e])
            def _():
                x_half_in(j, e).wait_recv()
                for i in range(len(RELAYS)):
                    from_relay(j, i).wait_recv()
                spread(e)

    def attend(j):
        for d in (0, 1):
            pl.when(has_w[d])(lambda: q_in(j, d).wait_recv())
        for d in (0, 1):
            @pl.when(has_t[d])
            def _():
                waits = jnp.logical_not(is_inner & (off == d)) if INNER else True
                pl.when(waits)(lambda: t_in(j, d, 1).wait_recv())
                for e in (0, 1):
                    pl.when(has_h[e])(lambda: t_in(j, d, 2 * e).wait_recv())

        @pl.loop(0, GROUP)
        def _(g):
            for k in (0, 1):
                queries = qb[j, g, k].reshape(3 * TILE, HEAD_DIM)
                keys = kv[j, g, k : k + 3, :, 0].reshape(9 * TILE, HEAD_DIM)
                values = kv[j, g, k : k + 3, :, 1].reshape(9 * TILE, HEAD_DIM)
                counted = valid[k : k + 3].reshape(9 * TILE, HEAD_DIM)
                scores = lax.dot_general(
                    queries, keys, (((1,), (1,)), ((), ())), preferred_element_type=jnp.float32
                )
                highest = jnp.max(scores, axis=1, keepdims=True)
                weights = jnp.exp2((scores - highest) * SCALE).astype(jnp.bfloat16)
                blended = jnp.dot(
                    weights, jnp.concatenate([values, counted], axis=1), preferred_element_type=jnp.float32
                )
                totals = blended[:, HEAD_DIM:]
                part = blended[:, :HEAD_DIM] / totals
                level = highest * SCALE + jnp.log2(totals)
                own_o[j, g, k] = part[TILE : 2 * TILE]
                own_l[j, g, k] = level[TILE : 2 * TILE]
                for d in (0, 1):
                    at = slice(2 * d * TILE, (2 * d + 1) * TILE)
                    osend[j, d, g, k] = part[at].astype(jnp.bfloat16)
                    ssend[j, d, g, k : k + 1] = jnp.sum(jnp.where(diagonal, level[at], 0.0), axis=0, keepdims=True)

        for d in (0, 1):
            @pl.when(has_w[d])
            def _():
                o_copy(j, d).start()
                s_copy(j, d).start()

    def combine(j):
        for d in (0, 1):
            @pl.when(has_w[d])
            def _():
                o_in(j, d).wait_recv()
                s_in(j, d).wait_recv()
        @pl.loop(0, GROUP)
        def _(g):
            for k in (0, 1):
                levels = [own_l[j, g, k]]
                for d in (0, 1):
                    row = jnp.broadcast_to(srecv[j, d, g, k : k + 1], (TILE, HEAD_DIM))
                    levels.append(jnp.sum(jnp.where(diagonal, row, 0.0), axis=1, keepdims=True))
                top = jnp.maximum(jnp.maximum(levels[1], levels[2]), levels[0])
                shares = [jnp.exp2(level - top) for level in levels]
                mixed = shares[0] * own_o[j, g, k]
                for d in (0, 1):
                    mixed += shares[1 + d] * orecv[j, d, g, k].astype(jnp.float32)
                at = pl.ds(pl.multiple_of((j * GROUP + g) * HEAD_DIM, HEAD_DIM), HEAD_DIM)
                result = (mixed / (shares[0] + shares[1] + shares[2])).astype(jnp.bfloat16)
                outb[TT * k : TT * (k + 1), :, :, at] = result.reshape(TT, TH, TW, HEAD_DIM)

    pl.loop(0, LEAD)(pass_on)

    @pl.loop(0, groups + BEHIND)
    def _(step):
        pl.when(step + FAR_AHEAD < groups)(lambda: launch_far(step + FAR_AHEAD))
        pl.when(step + LEAD < groups)(lambda: pass_on(step + LEAD))
        pl.when(step + AHEAD < groups)(lambda: launch(step + AHEAD))
        pl.when(step < groups)(lambda: forward(step))
        pl.when((step >= 1) & (step <= groups))(lambda: attend(step - 1))
        pl.when(step >= BEHIND)(lambda: combine(step - BEHIND))

    every = slice(None)
    for i in range(len(RELAYS)):
        pl.when(is_relay[i])(lambda: relay_out(every, i).wait_send())
    if INNER:
        pl.when(is_inner & has_off)(lambda: edge_copy(every).wait_send())
    for d in (0, 1):
        @pl.when(far[d])
        def _():
            for i in range(len(RELAYS)):
                to_relay(every, i).wait_send()
            x_half(every, d).wait_send()

        pl.when(has_h[d] & jnp.logical_not(far[d]))(lambda: x_copy(every, d).wait_send())

        @pl.when(has_t[d])
        def _():
            t_copy(every, d, 1).wait_send()
            for e in (0, 1):
                pl.when(has_h[e] & spreads(d, e))(lambda: t_copy(every, d, 2 * e).wait_send())

        @pl.when(has_w[d])
        def _():
            q_copy(every, d).wait_send()
            o_copy(every, d).wait_send()
            s_copy(every, d).wait_send()


def body(queries, keys, values):
    groups = queries.shape[3] // HEAD_DIM // GROUP
    bf16, f32 = jnp.bfloat16, jnp.float32
    dma = pltpu.SemaphoreType.DMA
    own = pltpu.VMEM(queries.shape, jnp.bfloat16)
    return pl.pallas_call(
        functools.partial(kernel, groups),
        out_shape=jax.ShapeDtypeStruct(queries.shape, bf16),
        in_specs=[pl.BlockSpec(memory_space=pl.ANY)] * 3,
        out_specs=pl.BlockSpec(memory_space=pltpu.VMEM),
        scratch_shapes=[
            own, own, own,
            pltpu.VMEM((groups, GROUP, 2, 3, TILE, HEAD_DIM), bf16),
            pltpu.VMEM((groups, GROUP, 4, 3, 2, TILE, HEAD_DIM), bf16),
            pltpu.VMEM((4, 3, TILE, HEAD_DIM), bf16),
            pltpu.VMEM((groups, 2, GROUP, 2, TILE, HEAD_DIM), bf16),
            pltpu.VMEM((groups, 2, GROUP, 2, TILE, HEAD_DIM), bf16),
            pltpu.VMEM((groups, 2, GROUP, 8, HEAD_DIM), f32),
            pltpu.VMEM((groups, 2, GROUP, 8, HEAD_DIM), f32),
            pltpu.VMEM((groups, GROUP, 2, TILE, HEAD_DIM), f32),
            pltpu.VMEM((groups, GROUP, 2, TILE, HEAD_DIM), f32),
            pltpu.VMEM((groups, GROUP, 2, 2, max(SHARES[1:]), HEAD_DIM), bf16),
            dma((3,)), dma((1,)),
            dma((2,)), dma((groups, 2)),
            dma((2, 3)), dma((groups, 2, 3)),
            dma((2,)), dma((groups, 2)),
            dma((2,)), dma((groups, 2)),
            dma((2,)), dma((groups, 2)),
            dma((len(RELAYS),)), dma((groups,)), dma((len(RELAYS),)), dma((groups, len(RELAYS))),
        ],
        compiler_params=pltpu.CompilerParams(
            collective_id=0, has_side_effects=True, vmem_limit_bytes=63 * 2**20
        ),
        name="window_attention",
    )(queries, keys, values)


def solution(mesh):
    placed = (P("ta", "ha", "wa", None),) * 3
    return jax.shard_map(
        body, mesh=mesh, in_specs=placed, out_specs=P("ta", "ha", "wa", None), check_vma=False
    )
```

```python
import functools
import math

import jax
import jax.numpy as jnp
from jax import lax
from jax.experimental import pallas as pl
from jax.experimental.pallas import tpu as pltpu
from jax.sharding import PartitionSpec as P

HEAD_DIM = 128
TT, TH, TW = 6, 4, 4
TILE = TT * TH * TW
MESH = pl.DeviceIdType.MESH
SCALE = HEAD_DIM**-0.5 * math.log2(math.e)
SHARES = (32, 32, 16, 16)
RELAYS = (0, 2, 1)
INNER = False
GROUP = 3
AHEAD = 2
FAR_AHEAD = 3
LEAD = 1
BEHIND = 2


def kernel(
    groups, q_hbm, k_hbm, v_hbm, outb,
    q_own, k_own, v_own, qb, kv, valid, osend, orecv, ssend, srecv, own_o, own_l,
    passing, load, es, xs, xr, ts, tr, qs, qr, os_, or_, ss, sr, ps, pr, fs, fr,
):
    t, h, w = lax.axis_index("ta"), lax.axis_index("ha"), lax.axis_index("wa")
    nt, nh, nw = lax.axis_size("ta"), lax.axis_size("ha"), lax.axis_size("wa")
    has_t = (t > 0, t < nt - 1)
    has_h = (h > 0, h < nh - 1)
    has_w = (w > 0, w < nw - 1)
    near_t = ((t - 1, h, w), (t + 1, h, w))
    near_h = ((t, h - 1, w), (t, h + 1, w))
    near_w = ((t, h, w - 1), (t, h, w + 1))
    low, high = nh // 2 - 1, nh // 2
    far = (h == high, h == low)
    is_far = (h == low) | (h == high)
    lower = h <= low
    relays = [(t, jnp.where(h == low, r, nh - 1 - r), w) for r in RELAYS]
    other_relays = [(t, jnp.where(h == low, nh - 1 - r, r), w) for r in RELAYS]
    is_relay = [(h == r) | (h == nh - 1 - r) for r in RELAYS]
    relay_from = (t, jnp.where(lower, low, high), w)
    relay_to = (t, jnp.where(lower, high, low), w)
    shares = [pl.ds(sum(SHARES[:i]), size) for i, size in enumerate(SHARES)]
    far_slot = jnp.where(h == low, 2, 0)
    relay_slot = jnp.where(lower, 0, 2)

    off = lax.rem(t, 2)
    has_off = (off == 0) & has_t[0] | (off == 1) & has_t[1]
    is_inner = (h == low - 1) | (h == high + 1)
    inner_slot = jnp.where(h == low - 1, 0, 2)
    inner_to = (t, jnp.where(h == low - 1, low, high), w)

    def remote(src, dst, send, recv, device):
        return pltpu.make_async_remote_copy(src, dst, send, recv, device_id=device, device_id_type=MESH)

    def nth(j):
        return 0 if isinstance(j, slice) else j

    def x_copy(j, d):
        return remote(kv.at[j, :, 1:3, 1], kv.at[j, :, 1:3, 0 if d else 2], xs.at[d], xr.at[nth(j), 1 - d], near_h[d])

    def x_half(j, d):
        return remote(
            kv.at[j, :, 1:3, 1, :, shares[0]], kv.at[j, :, 1:3, 0 if d else 2, :, shares[0]],
            xs.at[d], xr.at[nth(j), 1 - d], near_h[d],
        )

    def held(j, i):
        return passing.at[j, :, :, :, pl.ds(0, SHARES[1 + i])]

    def to_relay(j, i):
        return remote(kv.at[j, :, 1:3, 1, :, shares[1 + i]], held(j, i), ps.at[i], pr.at[nth(j)], relays[i])

    def relay_in(j, i):
        return remote(kv.at[j, :, 1:3, 1, :, shares[1 + i]], held(j, i), ps.at[i], pr.at[nth(j)], relay_from)

    def relay_out(j, i):
        return remote(
            held(j, i), kv.at[j, :, 1:3, relay_slot, :, shares[1 + i]], fs.at[i], fr.at[nth(j), i], relay_to
        )

    def from_relay(j, i):
        return remote(
            held(j, i), kv.at[j, :, 1:3, far_slot, :, shares[1 + i]], fs.at[i], fr.at[nth(j), i], other_relays[i]
        )

    def t_copy(j, d, hh):
        return remote(kv.at[j, :, 1 + d, hh], kv.at[j, :, 0 if d else 3, hh], ts.at[d, hh], tr.at[nth(j), 1 - d, hh], near_t[d])

    def edge_copy(j):
        return remote(
            kv.at[j, :, 3 * off, 1], kv.at[j, :, 3 * off, inner_slot], es.at[0], tr.at[nth(j), off, inner_slot], inner_to
        )

    def q_copy(j, d):
        return remote(qb.at[j, :, :, 1], qb.at[j, :, :, 0 if d else 2], qs.at[d], qr.at[nth(j), 1 - d], near_w[d])

    def o_copy(j, d, g):
        return remote(osend.at[j, d, g], orecv.at[j, 1 - d, g], os_.at[d], or_.at[nth(j), nth(g), 1 - d], near_w[d])

    def s_copy(j, d, g):
        return remote(ssend.at[j, d, g], srecv.at[j, 1 - d, g], ss.at[d], sr.at[nth(j), nth(g), 1 - d], near_w[d])

    def x_in(j, d):
        return remote(kv.at[j, :, 1:3, 1], kv.at[j, :, 1:3, 2 * d], xs.at[d], xr.at[nth(j), d], near_h[d])

    def x_half_in(j, d):
        return remote(
            kv.at[j, :, 1:3, 1, :, shares[0]], kv.at[j, :, 1:3, 2 * d, :, shares[0]],
            xs.at[d], xr.at[nth(j), d], near_h[d],
        )

    def t_in(j, d, hh):
        return remote(kv.at[j, :, 1 + d, 1], kv.at[j, :, 3 * d, hh], ts.at[d, hh], tr.at[nth(j), d, hh], (t + 2 * d - 1, h, w))

    def q_in(j, d):
        return remote(qb.at[j, :, :, 1], qb.at[j, :, :, 2 * d], qs.at[d], qr.at[nth(j), d], near_w[d])

    def o_in(j, d, g):
        return remote(osend.at[j, d, g], orecv.at[j, d, g], os_.at[d], or_.at[nth(j), nth(g), d], near_w[d])

    def s_in(j, d, g):
        return remote(ssend.at[j, d, g], srecv.at[j, d, g], ss.at[d], sr.at[nth(j), nth(g), d], near_w[d])

    loads = [
        pltpu.make_async_copy(src, dst, load.at[i])
        for i, (src, dst) in enumerate(((k_hbm, k_own), (v_hbm, v_own), (q_hbm, q_own)))
    ]
    for copy in loads:
        copy.start()

    barrier = pltpu.get_barrier_semaphore()
    count = jnp.int32(0)
    for has, near in ((has_t, near_t), (has_h, near_h), (has_w, near_w)):
        for d in (0, 1):
            pl.when(has[d])(
                lambda near=near, d=d: pl.semaphore_signal(
                    barrier, inc=1, device_id=near[d], device_id_type=MESH
                )
            )
            count += has[d].astype(jnp.int32)
    greet = [(is_far, r) for r in relays + other_relays]
    greet += [(here, near) for here in is_relay for near in (relay_from, relay_to)]
    for here, near in greet:
        pl.when(here)(
            lambda near=near: pl.semaphore_signal(barrier, inc=1, device_id=near, device_id_type=MESH)
        )
        count += here.astype(jnp.int32)

    for tt in range(4):
        for hh in range(3):
            here = jnp.bool_(True)
            if tt in (0, 3):
                here = here & has_t[tt // 3]
            if hh in (0, 2):
                here = here & has_h[hh // 2]
            valid[tt, hh] = jnp.full((TILE, HEAD_DIM), here.astype(jnp.float32)).astype(jnp.bfloat16)
    for d in (0, 1):
        @pl.when(jnp.logical_not(has_w[d]))
        def _():
            qb[:, :, :, 2 * d] = jnp.zeros_like(qb[:, :, :, 2 * d])
            orecv[:, d] = jnp.zeros_like(orecv[:, d])
            srecv[:, d] = jnp.full_like(srecv[:, d], -1e30)

    def tiles(ref, j):
        at = pl.ds(pl.multiple_of(j * HEAD_DIM, HEAD_DIM), HEAD_DIM)
        return ref[:, :, :, at].reshape(2, TILE, HEAD_DIM)

    for copy in loads:
        copy.wait()

    none = jnp.zeros((TILE, HEAD_DIM), jnp.bfloat16)

    @pl.loop(0, groups)
    def _(j):
        @pl.loop(0, GROUP)
        def _(g):
            kv[j, g, 1:3, 1, 0] = tiles(k_own, j * GROUP + g)
            kv[j, g, 1:3, 1, 1] = tiles(v_own, j * GROUP + g)
            qb[j, g, :, 1] = tiles(q_own, j * GROUP + g)
            for e in (0, 1):
                @pl.when(jnp.logical_not(has_h[e]))
                def _():
                    for tt in range(4):
                        kv[j, g, tt, 2 * e, 0] = kv[j, g, 1 + tt // 2, 1, 0]
                        kv[j, g, tt, 2 * e, 1] = none
            for d in (0, 1):
                @pl.when(jnp.logical_not(has_t[d]))
                def _():
                    for hh in range(3):
                        kv[j, g, 3 * d, hh, 0] = kv[j, g, 1 + d, 1, 0]
                        kv[j, g, 3 * d, hh, 1] = none

    pl.semaphore_wait(barrier, count)

    def launch_far(j):
        for d in (0, 1):
            @pl.when(far[d])
            def _():
                for i in range(len(RELAYS)):
                    to_relay(j, i).start()
                x_half(j, d).start()

    def launch(j):
        for d in (0, 1):
            pl.when(has_h[d] & jnp.logical_not(far[d]))(lambda: x_copy(j, d).start())
        for d in (0, 1):
            pl.when(has_t[d])(lambda: t_copy(j, d, 1).start())
        for d in (0, 1):
            pl.when(has_w[d])(lambda: q_copy(j, d).start())

    pl.loop(0, FAR_AHEAD)(launch_far)
    pl.loop(0, AHEAD)(launch)

    rows = lax.broadcasted_iota(jnp.int32, (TILE, HEAD_DIM), 0)
    lanes = lax.broadcasted_iota(jnp.int32, (TILE, HEAD_DIM), 1)
    diagonal = rows == lanes

    def spreads(d, e):
        return has_t[d] & jnp.logical_not((off == d) & far[1 - e]) if INNER else has_t[d]

    def pass_on(j):
        for i in range(len(RELAYS)):
            @pl.when(is_relay[i])
            def _():
                relay_in(j, i).wait_recv()
                relay_out(j, i).start()

    def forward(j):

        if INNER:
            @pl.when(is_inner & has_off)
            def _():
                t_in(j, off, 1).wait_recv()
                edge_copy(j).start()

        def spread(e):
            for d in (0, 1):
                pl.when(spreads(d, e))(lambda: t_copy(j, d, 2 * e).start())

        for e in (0, 1):
            @pl.when(has_h[e] & jnp.logical_not(far[e]))
            def _():
                x_in(j, e).wait_recv()
                spread(e)
        for e in (0, 1):
            @pl.when(far[e])
            def _():
                x_half_in(j, e).wait_recv()
                for i in range(len(RELAYS)):
                    from_relay(j, i).wait_recv()
                spread(e)

    def attend(j):
        for d in (0, 1):
            pl.when(has_w[d])(lambda: q_in(j, d).wait_recv())
        for d in (0, 1):
            @pl.when(has_t[d])
            def _():
                waits = jnp.logical_not(is_inner & (off == d)) if INNER else True
                pl.when(waits)(lambda: t_in(j, d, 1).wait_recv())
                for e in (0, 1):
                    pl.when(has_h[e])(lambda: t_in(j, d, 2 * e).wait_recv())

        @pl.loop(0, GROUP)
        def _(g):
            for k in (0, 1):
                queries = qb[j, g, k].reshape(3 * TILE, HEAD_DIM)
                keys = kv[j, g, k : k + 3, :, 0].reshape(9 * TILE, HEAD_DIM)
                values = kv[j, g, k : k + 3, :, 1].reshape(9 * TILE, HEAD_DIM)
                counted = valid[k : k + 3].reshape(9 * TILE, HEAD_DIM)
                scores = lax.dot_general(
                    queries, keys, (((1,), (1,)), ((), ())), preferred_element_type=jnp.float32
                )
                highest = jnp.max(scores, axis=1, keepdims=True)
                weights = jnp.exp2((scores - highest) * SCALE).astype(jnp.bfloat16)
                blended = jnp.dot(
                    weights, jnp.concatenate([values, counted], axis=1), preferred_element_type=jnp.float32
                )
                totals = blended[:, HEAD_DIM:]
                part = blended[:, :HEAD_DIM] / totals
                level = highest * SCALE + jnp.log2(totals)
                own_o[j, g, k] = part[TILE : 2 * TILE]
                own_l[j, g, k] = level[TILE : 2 * TILE]
                for d in (0, 1):
                    at = slice(2 * d * TILE, (2 * d + 1) * TILE)
                    osend[j, d, g, k] = part[at].astype(jnp.bfloat16)
                    ssend[j, d, g, k : k + 1] = jnp.sum(jnp.where(diagonal, level[at], 0.0), axis=0, keepdims=True)
            for d in (0, 1):
                @pl.when(has_w[d])
                def _():
                    o_copy(j, d, g).start()
                    s_copy(j, d, g).start()

    def combine(j):
        @pl.loop(0, GROUP)
        def _(g):
            for d in (0, 1):
                @pl.when(has_w[d])
                def _():
                    o_in(j, d, g).wait_recv()
                    s_in(j, d, g).wait_recv()
            for k in (0, 1):
                levels = [own_l[j, g, k]]
                for d in (0, 1):
                    row = jnp.broadcast_to(srecv[j, d, g, k : k + 1], (TILE, HEAD_DIM))
                    levels.append(jnp.sum(jnp.where(diagonal, row, 0.0), axis=1, keepdims=True))
                top = jnp.maximum(jnp.maximum(levels[1], levels[2]), levels[0])
                shares = [jnp.exp2(level - top) for level in levels]
                mixed = shares[0] * own_o[j, g, k]
                for d in (0, 1):
                    mixed += shares[1 + d] * orecv[j, d, g, k].astype(jnp.float32)
                at = pl.ds(pl.multiple_of((j * GROUP + g) * HEAD_DIM, HEAD_DIM), HEAD_DIM)
                result = (mixed / (shares[0] + shares[1] + shares[2])).astype(jnp.bfloat16)
                outb[TT * k : TT * (k + 1), :, :, at] = result.reshape(TT, TH, TW, HEAD_DIM)

    pl.loop(0, LEAD)(pass_on)

    @pl.loop(0, groups + BEHIND)
    def _(step):
        pl.when(step + FAR_AHEAD < groups)(lambda: launch_far(step + FAR_AHEAD))
        pl.when(step + LEAD < groups)(lambda: pass_on(step + LEAD))
        pl.when(step + AHEAD < groups)(lambda: launch(step + AHEAD))
        pl.when(step < groups)(lambda: forward(step))
        pl.when((step >= 1) & (step <= groups))(lambda: attend(step - 1))
        pl.when(step >= BEHIND)(lambda: combine(step - BEHIND))

    every = slice(None)
    for i in range(len(RELAYS)):
        pl.when(is_relay[i])(lambda: relay_out(every, i).wait_send())
    if INNER:
        pl.when(is_inner & has_off)(lambda: edge_copy(every).wait_send())
    for d in (0, 1):
        @pl.when(far[d])
        def _():
            for i in range(len(RELAYS)):
                to_relay(every, i).wait_send()
            x_half(every, d).wait_send()

        pl.when(has_h[d] & jnp.logical_not(far[d]))(lambda: x_copy(every, d).wait_send())

        @pl.when(has_t[d])
        def _():
            t_copy(every, d, 1).wait_send()
            for e in (0, 1):
                pl.when(has_h[e] & spreads(d, e))(lambda: t_copy(every, d, 2 * e).wait_send())

        @pl.when(has_w[d])
        def _():
            q_copy(every, d).wait_send()
            o_copy(every, d, every).wait_send()
            s_copy(every, d, every).wait_send()


def body(queries, keys, values):
    groups = queries.shape[3] // HEAD_DIM // GROUP
    bf16, f32 = jnp.bfloat16, jnp.float32
    dma = pltpu.SemaphoreType.DMA
    own = pltpu.VMEM(queries.shape, jnp.bfloat16)
    return pl.pallas_call(
        functools.partial(kernel, groups),
        out_shape=jax.ShapeDtypeStruct(queries.shape, bf16),
        in_specs=[pl.BlockSpec(memory_space=pl.ANY)] * 3,
        out_specs=pl.BlockSpec(memory_space=pltpu.VMEM),
        scratch_shapes=[
            own, own, own,
            pltpu.VMEM((groups, GROUP, 2, 3, TILE, HEAD_DIM), bf16),
            pltpu.VMEM((groups, GROUP, 4, 3, 2, TILE, HEAD_DIM), bf16),
            pltpu.VMEM((4, 3, TILE, HEAD_DIM), bf16),
            pltpu.VMEM((groups, 2, GROUP, 2, TILE, HEAD_DIM), bf16),
            pltpu.VMEM((groups, 2, GROUP, 2, TILE, HEAD_DIM), bf16),
            pltpu.VMEM((groups, 2, GROUP, 8, HEAD_DIM), f32),
            pltpu.VMEM((groups, 2, GROUP, 8, HEAD_DIM), f32),
            pltpu.VMEM((groups, GROUP, 2, TILE, HEAD_DIM), f32),
            pltpu.VMEM((groups, GROUP, 2, TILE, HEAD_DIM), f32),
            pltpu.VMEM((groups, GROUP, 2, 2, max(SHARES[1:]), HEAD_DIM), bf16),
            dma((3,)), dma((1,)),
            dma((2,)), dma((groups, 2)),
            dma((2, 3)), dma((groups, 2, 3)),
            dma((2,)), dma((groups, 2)),
            dma((2,)), dma((groups, GROUP, 2)),
            dma((2,)), dma((groups, GROUP, 2)),
            dma((len(RELAYS),)), dma((groups,)), dma((len(RELAYS),)), dma((groups, len(RELAYS))),
        ],
        compiler_params=pltpu.CompilerParams(
            collective_id=0, has_side_effects=True, vmem_limit_bytes=53 * 2**20 + 2**17
        ),
        name="window_attention",
    )(queries, keys, values)


def solution(mesh):
    placed = (P("ta", "ha", "wa", None),) * 3
    return jax.shard_map(
        body, mesh=mesh, in_specs=placed, out_specs=P("ta", "ha", "wa", None), check_vma=False
    )
```

```python
import functools
import math

import jax
import jax.numpy as jnp
from jax import lax
from jax.experimental import pallas as pl
from jax.experimental.pallas import tpu as pltpu
from jax.sharding import PartitionSpec as P

HEAD_DIM = 128
TT, TH, TW = 6, 4, 4
TILE = TT * TH * TW
MESH = pl.DeviceIdType.MESH
SCALE = HEAD_DIM**-0.5 * math.log2(math.e)
SHARES = (32, 32, 16, 16)
RELAYS = (0, 2, 1)
INNER = False
GROUP = 3
AHEAD = 3
FAR_AHEAD = 4
LEAD = 1
BEHIND = 2


def kernel(
    groups, q_hbm, k_hbm, v_hbm, outb,
    q_own, k_own, v_own, qb, kv, valid, osend, orecv, ssend, srecv, own_o, own_l,
    passing, load, es, xs, xr, ts, tr, qs, qr, os_, or_, ss, sr, ps, pr, fs, fr,
):
    t, h, w = lax.axis_index("ta"), lax.axis_index("ha"), lax.axis_index("wa")
    nt, nh, nw = lax.axis_size("ta"), lax.axis_size("ha"), lax.axis_size("wa")
    has_t = (t > 0, t < nt - 1)
    has_h = (h > 0, h < nh - 1)
    has_w = (w > 0, w < nw - 1)
    near_t = ((t - 1, h, w), (t + 1, h, w))
    near_h = ((t, h - 1, w), (t, h + 1, w))
    near_w = ((t, h, w - 1), (t, h, w + 1))
    low, high = nh // 2 - 1, nh // 2
    far = (h == high, h == low)
    is_far = (h == low) | (h == high)
    lower = h <= low
    relays = [(t, jnp.where(h == low, r, nh - 1 - r), w) for r in RELAYS]
    other_relays = [(t, jnp.where(h == low, nh - 1 - r, r), w) for r in RELAYS]
    is_relay = [(h == r) | (h == nh - 1 - r) for r in RELAYS]
    relay_from = (t, jnp.where(lower, low, high), w)
    relay_to = (t, jnp.where(lower, high, low), w)
    shares = [pl.ds(sum(SHARES[:i]), size) for i, size in enumerate(SHARES)]
    far_slot = jnp.where(h == low, 2, 0)
    relay_slot = jnp.where(lower, 0, 2)

    off = lax.rem(t, 2)
    has_off = (off == 0) & has_t[0] | (off == 1) & has_t[1]
    is_inner = (h == low - 1) | (h == high + 1)
    inner_slot = jnp.where(h == low - 1, 0, 2)
    inner_to = (t, jnp.where(h == low - 1, low, high), w)

    def remote(src, dst, send, recv, device):
        return pltpu.make_async_remote_copy(src, dst, send, recv, device_id=device, device_id_type=MESH)

    def nth(j):
        return 0 if isinstance(j, slice) else j

    def x_copy(j, d):
        return remote(kv.at[j, :, 1:3, 1], kv.at[j, :, 1:3, 0 if d else 2], xs.at[d], xr.at[nth(j), 1 - d], near_h[d])

    def x_half(j, d):
        return remote(
            kv.at[j, :, 1:3, 1, :, shares[0]], kv.at[j, :, 1:3, 0 if d else 2, :, shares[0]],
            xs.at[d], xr.at[nth(j), 1 - d], near_h[d],
        )

    def held(j, i):
        return passing.at[j, :, :, :, pl.ds(0, SHARES[1 + i])]

    def to_relay(j, i):
        return remote(kv.at[j, :, 1:3, 1, :, shares[1 + i]], held(j, i), ps.at[i], pr.at[nth(j)], relays[i])

    def relay_in(j, i):
        return remote(kv.at[j, :, 1:3, 1, :, shares[1 + i]], held(j, i), ps.at[i], pr.at[nth(j)], relay_from)

    def relay_out(j, i):
        return remote(
            held(j, i), kv.at[j, :, 1:3, relay_slot, :, shares[1 + i]], fs.at[i], fr.at[nth(j), i], relay_to
        )

    def from_relay(j, i):
        return remote(
            held(j, i), kv.at[j, :, 1:3, far_slot, :, shares[1 + i]], fs.at[i], fr.at[nth(j), i], other_relays[i]
        )

    def t_copy(j, d, hh):
        return remote(kv.at[j, :, 1 + d, hh], kv.at[j, :, 0 if d else 3, hh], ts.at[d, hh], tr.at[nth(j), 1 - d, hh], near_t[d])

    def edge_copy(j):
        return remote(
            kv.at[j, :, 3 * off, 1], kv.at[j, :, 3 * off, inner_slot], es.at[0], tr.at[nth(j), off, inner_slot], inner_to
        )

    def q_copy(j, d):
        return remote(qb.at[j, :, :, 1], qb.at[j, :, :, 0 if d else 2], qs.at[d], qr.at[nth(j), 1 - d], near_w[d])

    def o_copy(j, d, g):
        return remote(osend.at[j, d, g], orecv.at[j, 1 - d, g], os_.at[d], or_.at[nth(j), nth(g), 1 - d], near_w[d])

    def s_copy(j, d, g):
        return remote(ssend.at[j, d, g], srecv.at[j, 1 - d, g], ss.at[d], sr.at[nth(j), nth(g), 1 - d], near_w[d])

    def x_in(j, d):
        return remote(kv.at[j, :, 1:3, 1], kv.at[j, :, 1:3, 2 * d], xs.at[d], xr.at[nth(j), d], near_h[d])

    def x_half_in(j, d):
        return remote(
            kv.at[j, :, 1:3, 1, :, shares[0]], kv.at[j, :, 1:3, 2 * d, :, shares[0]],
            xs.at[d], xr.at[nth(j), d], near_h[d],
        )

    def t_in(j, d, hh):
        return remote(kv.at[j, :, 1 + d, 1], kv.at[j, :, 3 * d, hh], ts.at[d, hh], tr.at[nth(j), d, hh], (t + 2 * d - 1, h, w))

    def q_in(j, d):
        return remote(qb.at[j, :, :, 1], qb.at[j, :, :, 2 * d], qs.at[d], qr.at[nth(j), d], near_w[d])

    def o_in(j, d, g):
        return remote(osend.at[j, d, g], orecv.at[j, d, g], os_.at[d], or_.at[nth(j), nth(g), d], near_w[d])

    def s_in(j, d, g):
        return remote(ssend.at[j, d, g], srecv.at[j, d, g], ss.at[d], sr.at[nth(j), nth(g), d], near_w[d])

    loads = [
        pltpu.make_async_copy(src, dst, load.at[i])
        for i, (src, dst) in enumerate(((k_hbm, k_own), (v_hbm, v_own), (q_hbm, q_own)))
    ]
    for copy in loads:
        copy.start()

    barrier = pltpu.get_barrier_semaphore()
    count = jnp.int32(0)
    for has, near in ((has_t, near_t), (has_h, near_h), (has_w, near_w)):
        for d in (0, 1):
            pl.when(has[d])(
                lambda near=near, d=d: pl.semaphore_signal(
                    barrier, inc=1, device_id=near[d], device_id_type=MESH
                )
            )
            count += has[d].astype(jnp.int32)
    greet = [(is_far, r) for r in relays + other_relays]
    greet += [(here, near) for here in is_relay for near in (relay_from, relay_to)]
    for here, near in greet:
        pl.when(here)(
            lambda near=near: pl.semaphore_signal(barrier, inc=1, device_id=near, device_id_type=MESH)
        )
        count += here.astype(jnp.int32)

    for tt in range(4):
        for hh in range(3):
            here = jnp.bool_(True)
            if tt in (0, 3):
                here = here & has_t[tt // 3]
            if hh in (0, 2):
                here = here & has_h[hh // 2]
            valid[tt, hh] = jnp.full((TILE, HEAD_DIM), here.astype(jnp.float32)).astype(jnp.bfloat16)
    for d in (0, 1):
        @pl.when(jnp.logical_not(has_w[d]))
        def _():
            qb[:, :, :, 2 * d] = jnp.zeros_like(qb[:, :, :, 2 * d])
            orecv[:, d] = jnp.zeros_like(orecv[:, d])
            srecv[:, d] = jnp.full_like(srecv[:, d], -1e30)

    def tiles(ref, j):
        at = pl.ds(pl.multiple_of(j * HEAD_DIM, HEAD_DIM), HEAD_DIM)
        return ref[:, :, :, at].reshape(2, TILE, HEAD_DIM)

    for copy in loads:
        copy.wait()

    none = jnp.zeros((TILE, HEAD_DIM), jnp.bfloat16)

    @pl.loop(0, groups)
    def _(j):
        @pl.loop(0, GROUP)
        def _(g):
            kv[j, g, 1:3, 1, 0] = tiles(k_own, j * GROUP + g)
            kv[j, g, 1:3, 1, 1] = tiles(v_own, j * GROUP + g)
            qb[j, g, :, 1] = tiles(q_own, j * GROUP + g)
            for e in (0, 1):
                @pl.when(jnp.logical_not(has_h[e]))
                def _():
                    for tt in range(4):
                        kv[j, g, tt, 2 * e, 0] = kv[j, g, 1 + tt // 2, 1, 0]
                        kv[j, g, tt, 2 * e, 1] = none
            for d in (0, 1):
                @pl.when(jnp.logical_not(has_t[d]))
                def _():
                    for hh in range(3):
                        kv[j, g, 3 * d, hh, 0] = kv[j, g, 1 + d, 1, 0]
                        kv[j, g, 3 * d, hh, 1] = none

    pl.semaphore_wait(barrier, count)

    def launch_far(j):
        for d in (0, 1):
            @pl.when(far[d])
            def _():
                for i in range(len(RELAYS)):
                    to_relay(j, i).start()
                x_half(j, d).start()

    def launch(j):
        for d in (0, 1):
            pl.when(has_h[d] & jnp.logical_not(far[d]))(lambda: x_copy(j, d).start())
        for d in (0, 1):
            pl.when(has_t[d])(lambda: t_copy(j, d, 1).start())
        for d in (0, 1):
            pl.when(has_w[d])(lambda: q_copy(j, d).start())

    pl.loop(0, FAR_AHEAD)(launch_far)
    pl.loop(0, AHEAD)(launch)

    rows = lax.broadcasted_iota(jnp.int32, (TILE, HEAD_DIM), 0)
    lanes = lax.broadcasted_iota(jnp.int32, (TILE, HEAD_DIM), 1)
    diagonal = rows == lanes

    def spreads(d, e):
        return has_t[d] & jnp.logical_not((off == d) & far[1 - e]) if INNER else has_t[d]

    def pass_on(j):
        for i in range(len(RELAYS)):
            @pl.when(is_relay[i])
            def _():
                relay_in(j, i).wait_recv()
                relay_out(j, i).start()

    def forward(j):

        if INNER:
            @pl.when(is_inner & has_off)
            def _():
                t_in(j, off, 1).wait_recv()
                edge_copy(j).start()

        def spread(e):
            for d in (0, 1):
                pl.when(spreads(d, e))(lambda: t_copy(j, d, 2 * e).start())

        for e in (0, 1):
            @pl.when(has_h[e] & jnp.logical_not(far[e]))
            def _():
                x_in(j, e).wait_recv()
                spread(e)
        for e in (0, 1):
            @pl.when(far[e])
            def _():
                x_half_in(j, e).wait_recv()
                for i in range(len(RELAYS)):
                    from_relay(j, i).wait_recv()
                spread(e)

    def attend(j):
        for d in (0, 1):
            pl.when(has_w[d])(lambda: q_in(j, d).wait_recv())
        for d in (0, 1):
            @pl.when(has_t[d])
            def _():
                waits = jnp.logical_not(is_inner & (off == d)) if INNER else True
                pl.when(waits)(lambda: t_in(j, d, 1).wait_recv())
                for e in (0, 1):
                    pl.when(has_h[e])(lambda: t_in(j, d, 2 * e).wait_recv())

        @pl.loop(0, GROUP)
        def _(g):
            for k in (0, 1):
                queries = qb[j, g, k].reshape(3 * TILE, HEAD_DIM)
                keys = kv[j, g, k : k + 3, :, 0].reshape(9 * TILE, HEAD_DIM)
                values = kv[j, g, k : k + 3, :, 1].reshape(9 * TILE, HEAD_DIM)
                counted = valid[k : k + 3].reshape(9 * TILE, HEAD_DIM)
                scores = lax.dot_general(
                    queries, keys, (((1,), (1,)), ((), ())), preferred_element_type=jnp.float32
                )
                highest = jnp.max(scores, axis=1, keepdims=True)
                weights = jnp.exp2((scores - highest) * SCALE).astype(jnp.bfloat16)
                blended = jnp.dot(
                    weights, jnp.concatenate([values, counted], axis=1), preferred_element_type=jnp.float32
                )
                totals = blended[:, HEAD_DIM:]
                part = blended[:, :HEAD_DIM] / totals
                level = highest * SCALE + jnp.log2(totals)
                own_o[j, g, k] = part[TILE : 2 * TILE]
                own_l[j, g, k] = level[TILE : 2 * TILE]
                for d in (0, 1):
                    at = slice(2 * d * TILE, (2 * d + 1) * TILE)
                    osend[j, d, g, k] = part[at].astype(jnp.bfloat16)
                    ssend[j, d, g, k : k + 1] = jnp.sum(jnp.where(diagonal, level[at], 0.0), axis=0, keepdims=True)
            for d in (0, 1):
                @pl.when(has_w[d])
                def _():
                    o_copy(j, d, g).start()
                    s_copy(j, d, g).start()

    def combine(j):
        @pl.loop(0, GROUP)
        def _(g):
            for d in (0, 1):
                @pl.when(has_w[d])
                def _():
                    o_in(j, d, g).wait_recv()
                    s_in(j, d, g).wait_recv()
            for k in (0, 1):
                levels = [own_l[j, g, k]]
                for d in (0, 1):
                    row = jnp.broadcast_to(srecv[j, d, g, k : k + 1], (TILE, HEAD_DIM))
                    levels.append(jnp.sum(jnp.where(diagonal, row, 0.0), axis=1, keepdims=True))
                top = jnp.maximum(jnp.maximum(levels[1], levels[2]), levels[0])
                shares = [jnp.exp2(level - top) for level in levels]
                mixed = shares[0] * own_o[j, g, k]
                for d in (0, 1):
                    mixed += shares[1 + d] * orecv[j, d, g, k].astype(jnp.float32)
                at = pl.ds(pl.multiple_of((j * GROUP + g) * HEAD_DIM, HEAD_DIM), HEAD_DIM)
                result = (mixed / (shares[0] + shares[1] + shares[2])).astype(jnp.bfloat16)
                outb[TT * k : TT * (k + 1), :, :, at] = result.reshape(TT, TH, TW, HEAD_DIM)

    pl.loop(0, LEAD)(pass_on)

    @pl.loop(0, groups + BEHIND)
    def _(step):
        pl.when(step + FAR_AHEAD < groups)(lambda: launch_far(step + FAR_AHEAD))
        pl.when(step + LEAD < groups)(lambda: pass_on(step + LEAD))
        pl.when(step + AHEAD < groups)(lambda: launch(step + AHEAD))
        pl.when(step < groups)(lambda: forward(step))
        pl.when((step >= 1) & (step <= groups))(lambda: attend(step - 1))
        pl.when(step >= BEHIND)(lambda: combine(step - BEHIND))

    every = slice(None)
    for i in range(len(RELAYS)):
        pl.when(is_relay[i])(lambda: relay_out(every, i).wait_send())
    if INNER:
        pl.when(is_inner & has_off)(lambda: edge_copy(every).wait_send())
    for d in (0, 1):
        @pl.when(far[d])
        def _():
            for i in range(len(RELAYS)):
                to_relay(every, i).wait_send()
            x_half(every, d).wait_send()

        pl.when(has_h[d] & jnp.logical_not(far[d]))(lambda: x_copy(every, d).wait_send())

        @pl.when(has_t[d])
        def _():
            t_copy(every, d, 1).wait_send()
            for e in (0, 1):
                pl.when(has_h[e] & spreads(d, e))(lambda: t_copy(every, d, 2 * e).wait_send())

        @pl.when(has_w[d])
        def _():
            q_copy(every, d).wait_send()
            o_copy(every, d, every).wait_send()
            s_copy(every, d, every).wait_send()


def body(queries, keys, values):
    groups = queries.shape[3] // HEAD_DIM // GROUP
    bf16, f32 = jnp.bfloat16, jnp.float32
    dma = pltpu.SemaphoreType.DMA
    own = pltpu.VMEM(queries.shape, jnp.bfloat16)
    return pl.pallas_call(
        functools.partial(kernel, groups),
        out_shape=jax.ShapeDtypeStruct(queries.shape, bf16),
        in_specs=[pl.BlockSpec(memory_space=pl.ANY)] * 3,
        out_specs=pl.BlockSpec(memory_space=pltpu.VMEM),
        scratch_shapes=[
            own, own, own,
            pltpu.VMEM((groups, GROUP, 2, 3, TILE, HEAD_DIM), bf16),
            pltpu.VMEM((groups, GROUP, 4, 3, 2, TILE, HEAD_DIM), bf16),
            pltpu.VMEM((4, 3, TILE, HEAD_DIM), bf16),
            pltpu.VMEM((groups, 2, GROUP, 2, TILE, HEAD_DIM), bf16),
            pltpu.VMEM((groups, 2, GROUP, 2, TILE, HEAD_DIM), bf16),
            pltpu.VMEM((groups, 2, GROUP, 8, HEAD_DIM), f32),
            pltpu.VMEM((groups, 2, GROUP, 8, HEAD_DIM), f32),
            pltpu.VMEM((groups, GROUP, 2, TILE, HEAD_DIM), f32),
            pltpu.VMEM((groups, GROUP, 2, TILE, HEAD_DIM), f32),
            pltpu.VMEM((groups, GROUP, 2, 2, max(SHARES[1:]), HEAD_DIM), bf16),
            dma((3,)), dma((1,)),
            dma((2,)), dma((groups, 2)),
            dma((2, 3)), dma((groups, 2, 3)),
            dma((2,)), dma((groups, 2)),
            dma((2,)), dma((groups, GROUP, 2)),
            dma((2,)), dma((groups, GROUP, 2)),
            dma((len(RELAYS),)), dma((groups,)), dma((len(RELAYS),)), dma((groups, len(RELAYS))),
        ],
        compiler_params=pltpu.CompilerParams(
            collective_id=0, has_side_effects=True, vmem_limit_bytes=53 * 2**20 + 2**17
        ),
        name="window_attention",
    )(queries, keys, values)


def solution(mesh):
    placed = (P("ta", "ha", "wa", None),) * 3
    return jax.shard_map(
        body, mesh=mesh, in_specs=placed, out_specs=P("ta", "ha", "wa", None), check_vma=False
    )
```
